1024 devices in a mesh: dp: 32 (over y, x), expert: 32 (over z, core).
Axes of the slice: x: 4, y: 8, z: 16, core: 2. Of those that a mesh axis runs over, the one named last changes fastest.
Arguments:
- tokens: bfloat16 [131072, 2048], P(('dp', 'expert')), may hold values from -6 to 6
- expert_ids: int32 [131072, 8], P(('dp', 'expert')), may hold values from 0 to 127, as said below
- gate_weights: float32 [131072, 8], P(('dp', 'expert')), may hold values from 0.1 to 1
- cotangent: bfloat16 [131072, 2048], P(('dp', 'expert')), may hold values from -3 to 3
- w_in: bfloat16 [2, 3072, 2048], P(None, 'expert'), may hold values from -0.125 to 0.125
- w_down: bfloat16 [3072, 2048], P('expert'), may hold values from -0.15625 to 0.15625
Outputs:
- moe_out: bfloat16 [131072, 2048], P(('dp', 'expert'))
- grad_tokens: bfloat16 [131072, 2048], P(('dp', 'expert'))
- grad_w_in: float32 [2, 3072, 2048], P(None, ('expert', 'dp'))
- grad_w_down: float32 [3072, 2048], P(('expert', 'dp'))
The draws below stay inside these ranges and needn't reach their ends.
Inputs may be any that keep to these rules, and one draw needn't show every extreme that they name: `expert_ids`: each token names 8 different experts, at most one of them below 2. In the 128 rows of one device no expert below 2 is named more than 8 times, and in every draw one expert below 2 is named exactly 8 times in the rows of every device.
All inputs are finite; a program needn't handle non-finite values.
Results may differ from the reference program's by a relative error of at most 0.02.
Values may be sent and summed in bfloat16 or wider, within the bound.
A program may use at most 32 MiB of HBM per device.

```python
import math
import jax
import jax.numpy as jnp
from jax import lax

D = 2048
FF = 1536
E_ALL = 128
TOP = 8
EXP_WIN = 2
CAP = 8
TOK_DEV = 128
TOKENS = 131072
SPLIT = 16
HID_DEV = 96
N_DP = 32
N_EXPERT = 32


def draw_expert_ids(key, part):
    key = jax.random.fold_in(key, 7)
    key_hot, key_count, key_place, key_rest, key_slot = jax.random.split(key, 5)
    blocks = TOKENS // TOK_DEV
    hot_expert = jax.random.randint(key_hot, (), 0, EXP_WIN)
    counts = jax.random.randint(key_count, (blocks, EXP_WIN), 1, CAP // 2 + 2)
    counts = jnp.where(jnp.arange(EXP_WIN)[None, :] == hot_expert, CAP, counts)
    bounds = jnp.cumsum(counts, axis=1)
    places = jnp.arange(TOK_DEV)
    window_id = jnp.sum((places[None, :, None] >= bounds[:, None, :]).astype(jnp.int32), axis=2)
    scores = jax.random.randint(key_place, (blocks, TOK_DEV), 0, 1 << 20) * TOK_DEV + places[None, :]
    shuffle = jnp.argsort(scores, axis=1)
    window_id = jnp.take_along_axis(window_id, shuffle, axis=1).reshape(TOKENS)
    id_range = jnp.arange(E_ALL)
    rest_scores = jax.random.randint(key_rest, (TOKENS, E_ALL), 0, 1 << 20) * E_ALL + id_range[None, :]
    rest_scores = jnp.where(id_range[None, :] < EXP_WIN, -1, rest_scores)
    picked = lax_top(rest_scores)
    has_window = window_id < EXP_WIN
    last_col = jnp.where(has_window, window_id, picked[:, TOP - 1])
    routed = jnp.concatenate([picked[:, :TOP - 1], last_col[:, None]], axis=1)
    slot_scores = jax.random.randint(key_slot, (TOKENS, TOP), 0, 1 << 20) * TOP + jnp.arange(TOP)[None, :]
    slot_order = jnp.argsort(slot_scores, axis=1)
    return jnp.take_along_axis(routed, slot_order, axis=1).astype(jnp.int32)


def lax_top(scores):
    return jax.lax.top_k(scores, TOP)[1].astype(jnp.int32)


def level_of(own_key, extent, cuts, smallest, largest):
    factor_of, own = 1.0, jax.random.fold_in(own_key, 6)
    for position, blocks in cuts:
        heights = jnp.exp(jax.random.uniform(jax.random.fold_in(own, position), (blocks,), jnp.float32, smallest / len(cuts), largest / len(cuts)))
        factor_of = factor_of * jnp.repeat(heights, extent[position] // blocks).reshape([-1 if axis == position else 1 for axis in range(len(extent))])
    return factor_of


def scatter_about(key, extent, deviation, bound, pieces=(), held_as=jnp.bfloat16):
    result = jax.random.normal(key, extent, jnp.float32) * deviation
    if len(pieces) > 0:
        result = level_of(key, extent, pieces, -0.22, 0.18) * result
    return jnp.clip(result, min=-bound, max=bound).astype(held_as)


def setup_inputs(seed: int = 0) -> dict:
    arg_keys = jax.random.split(jax.random.key(seed), 7)
    tokens = scatter_about(arg_keys[0], (TOKENS, D), 1.0, 6.0, ((0, 1024),))
    expert_ids = draw_expert_ids(jax.random.fold_in(arg_keys[6], 71), 0)
    gate_weights = jnp.clip(jnp.exp(math.log(1.0) - 2.3025851 * jax.random.uniform(arg_keys[2], (TOKENS, TOP), jnp.float32) ** level_of(arg_keys[2], (TOKENS, TOP), ((0, 1024),), -0.2, 0.2)), 0.1, 1.0)
    cotangent = scatter_about(arg_keys[3], (TOKENS, D), 0.5, 3.0, ((0, 1024),))
    w_in = scatter_about(arg_keys[4], (2, EXP_WIN * FF, D), D ** -0.5, 0.125, ((1, 32),))
    w_down = scatter_about(arg_keys[5], (EXP_WIN * FF, D), FF ** -0.5, 0.15625, ((0, 32),))
    return {"tokens": tokens, "expert_ids": expert_ids, "gate_weights": gate_weights, "cotangent": cotangent, "w_in": w_in, "w_down": w_down}


def silu_grad(preact):
    logistic = jax.nn.sigmoid(preact)
    return logistic * (1.0 + preact * (1.0 - logistic))

def settle(values):
    return lax.optimization_barrier(values.astype(jnp.bfloat16)).astype(jnp.float32)

def reference(tokens, expert_ids, gate_weights, cotangent, w_in, w_down):
    group_rows = N_EXPERT * TOK_DEV
    slot_total = N_EXPERT * CAP
    token_groups = tokens.reshape(N_DP, group_rows, D)
    id_groups = expert_ids.reshape(N_DP, group_rows, TOP)
    gate_groups = gate_weights.reshape(N_DP, group_rows, TOP)
    cotan_groups = cotangent.reshape(N_DP, group_rows, D)
    out_total = jnp.zeros((N_DP, group_rows, D), jnp.float32)
    grad_total = jnp.zeros((N_DP, group_rows, D), jnp.float32)
    gate_list, up_list, down_list = ([], [], [])
    for expert in range(EXP_WIN):
        w_gate = w_in[0, expert * FF:(expert + 1) * FF]
        w_up = w_in[1, expert * FF:(expert + 1) * FF]
        w_dn = w_down[expert * FF:(expert + 1) * FF]
        gate_sl = w_gate.astype(jnp.float32).reshape(SPLIT, HID_DEV, D)
        up_sl = w_up.astype(jnp.float32).reshape(SPLIT, HID_DEV, D)
        down_sl = w_dn.astype(jnp.float32).reshape(SPLIT, HID_DEV, D)

        def one_group(totals, inputs):
            token_block, id_block, gate_vals, cotan = inputs
            matches = id_block == expert
            chosen = jnp.any(matches, axis=1)
            weight = lax.optimization_barrier(jnp.sum(jnp.where(matches, gate_vals, 0.0), axis=1))
            row_index = jnp.nonzero(chosen, size=slot_total, fill_value=group_rows)[0].astype(jnp.int32)
            is_live = row_index < group_rows
            safe_index = jnp.minimum(row_index, group_rows - 1)
            row_tokens = jnp.where(is_live[:, None], token_block[safe_index], 0).astype(jnp.bfloat16)
            row_gates = jnp.where(is_live, weight[safe_index], 0.0)
            row_cotan = (row_gates[:, None] * cotan[safe_index].astype(jnp.float32)).astype(jnp.bfloat16)
            gate_pre = jnp.dot(row_tokens, w_gate.T, preferred_element_type=jnp.float32)
            up_pre = jnp.dot(row_tokens, w_up.T, preferred_element_type=jnp.float32)
            hidden = (jax.nn.silu(gate_pre) * up_pre).astype(jnp.bfloat16)
            hidden_sl = hidden.astype(jnp.float32).reshape(slot_total, SPLIT, HID_DEV)
            partial_value = settle(jnp.einsum('rsh,shd->rsd', hidden_sl, down_sl))
            out_rows = row_gates[:, None] * lax.optimization_barrier(jnp.sum(partial_value, axis=1))
            grad_hidden = jnp.dot(row_cotan, w_dn.T, preferred_element_type=jnp.float32)
            grad_gate = (grad_hidden * up_pre * silu_grad(gate_pre)).astype(jnp.bfloat16)
            grad_up = (grad_hidden * jax.nn.silu(gate_pre)).astype(jnp.bfloat16)
            gg_sl = grad_gate.astype(jnp.float32).reshape(slot_total, SPLIT, HID_DEV)
            gu_sl = grad_up.astype(jnp.float32).reshape(slot_total, SPLIT, HID_DEV)
            grad_part = settle(jnp.einsum('rsh,shd->rsd', gg_sl, gate_sl) + jnp.einsum('rsh,shd->rsd', gu_sl, up_sl))
            grad_rows = lax.optimization_barrier(jnp.sum(grad_part, axis=1))
            out_block = jnp.zeros((group_rows, D), jnp.float32).at[row_index].add(out_rows, mode='drop')
            grad_block = jnp.zeros((group_rows, D), jnp.float32).at[row_index].add(grad_rows, mode='drop')
            part_gate = settle(jnp.dot(grad_gate.T, row_tokens, preferred_element_type=jnp.float32))
            part_up = settle(jnp.dot(grad_up.T, row_tokens, preferred_element_type=jnp.float32))
            part_down = settle(jnp.dot(hidden.T, row_cotan, preferred_element_type=jnp.float32))
            totals = (totals[0] + part_gate, totals[1] + part_up, totals[2] + part_down)
            return (totals, (out_block, grad_block))
        zero_w = jnp.zeros((FF, D), jnp.float32)
        totals, blocks = lax.scan(one_group, (zero_w, zero_w, zero_w), (token_groups, id_groups, gate_groups, cotan_groups))
        out_total = out_total + blocks[0]
        grad_total = grad_total + blocks[1]
        gate_list.append(totals[0])
        up_list.append(totals[1])
        down_list.append(totals[2])
    moe_out = out_total.reshape(TOKENS, D).astype(jnp.bfloat16)
    grad_tokens = grad_total.reshape(TOKENS, D).astype(jnp.bfloat16)
    grad_w_in = jnp.stack([jnp.concatenate(gate_list, axis=0), jnp.concatenate(up_list, axis=0)], axis=0)
    grad_w_down = jnp.concatenate(down_list, axis=0)
    return (moe_out, grad_tokens, grad_w_in, grad_w_down)
```

```python
import functools

import jax
import jax.numpy as jnp
from jax import lax
from jax.experimental import pallas as pl
from jax.experimental.pallas import tpu as pltpu
from jax.sharding import PartitionSpec as P

MESH = pl.DeviceIdType.MESH
F32 = jnp.float32
BF16 = jnp.bfloat16
NT = (((1,), (1,)), ((), ()))
TN = (((0,), (0,)), ((), ()))


def moe_kernel(
    n_dp, nz,
    ids_ref, gates_ref, tok_hbm, cot_hbm, win_hbm, wdn_hbm,
    out_ref, gtok_ref, gwin_ref, gwdn_ref,
    tok, cot, win, wdn, x, pre, p32, q, qr, sb, rb, g32, g, rg, acc9,
    in_sem, ag_send, ag_recv, sib_send, sib_recv, q_send, q_recv,
    rs_send, rs_recv, g_send, g_recv,
):
    half = nz // 2
    feats = tok.shape[1]
    blocks = feats // 128
    hid = wdn.shape[0]
    per = hid // n_dp
    ntok = tok.shape[0]
    dp = lax.axis_index("dp")
    ex = lax.axis_index("expert")
    z = lax.div(ex, 2)
    core = lax.rem(ex, 2)
    zz = lax.rem(z, half)
    zl = half - 1 - zz
    held = lax.div(z, half)
    right = (dp, lax.rem(z + 1, nz) * 2 + core)
    left = (dp, lax.rem(z + nz - 1, nz) * 2 + core)
    sib = (dp, z * 2 + 1 - core)

    loads = [
        pltpu.make_async_copy(tok_hbm, tok, in_sem.at[0]),
        pltpu.make_async_copy(cot_hbm, cot, in_sem.at[1]),
        pltpu.make_async_copy(win_hbm, win, in_sem.at[2]),
        pltpu.make_async_copy(wdn_hbm, wdn, in_sem.at[3]),
    ]
    for load in loads:
        load.start()

    barrier = pltpu.get_barrier_semaphore()
    for dev in (right, left, sib):
        pl.semaphore_signal(barrier, inc=1, device_id=dev, device_id_type=MESH)

    @pl.loop(1, n_dp)
    def _(k):
        pl.semaphore_signal(
            barrier, inc=1, device_id=(lax.rem(dp + k, n_dp), ex), device_id_type=MESH
        )

    ids = ids_ref[...]
    gates = gates_ref[...]
    lane = lax.broadcasted_iota(jnp.int32, (ntok, ntok), 1)
    sub = lax.broadcasted_iota(jnp.int32, (ntok, ntok), 0)
    tri = jnp.where(lane < sub, 1.0, 0.0).astype(BF16)
    table = jnp.zeros((ntok, ntok), F32)
    for e in range(2):
        hit = ids == e
        chosen = jnp.max(jnp.where(hit, 1.0, 0.0), axis=1, keepdims=True)
        weight = jnp.sum(jnp.where(hit, gates, 0.0), axis=1, keepdims=True)
        table = jnp.where(lane == e, chosen, table)
        table = jnp.where(lane == 2 + e, weight, table)
    ranks = jnp.dot(tri, table.astype(BF16), preferred_element_type=F32)
    table_t = jnp.transpose(table)
    ranks_t = jnp.transpose(ranks)
    slot = lax.broadcasted_iota(jnp.int32, (8, ntok), 0).astype(F32)
    picks = []
    scales = []
    for e in range(2):
        pick = jnp.where(
            (table_t[e:e + 1] > 0.5) & (ranks_t[e:e + 1] == slot), 1.0, 0.0
        )
        picks.append(pick)
        scales.append(jnp.sum(pick * table_t[2 + e:3 + e], axis=1, keepdims=True))
    pick = jnp.concatenate(picks, axis=0).astype(BF16)
    scale = jnp.concatenate(scales, axis=0)

    loads[0].wait()
    tok_rows = jnp.dot(pick, tok[...], preferred_element_type=F32)
    loads[1].wait()
    cot_rows = jnp.dot(pick, cot[...], preferred_element_type=F32) * scale
    packet = [
        jnp.concatenate([tok_rows[8 * e:8 * e + 8], cot_rows[8 * e:8 * e + 8]], axis=0)
        for e in range(2)
    ]
    first = held == 0
    x[0, 0] = jnp.where(first, packet[0], packet[1]).astype(BF16)
    x[2, 0] = jnp.where(first, packet[1], packet[0]).astype(BF16)

    pl.semaphore_wait(barrier, 3 + n_dp - 1)

    def slot_r(i):
        return 2 * i - 1 if i > 0 else 0

    def slot_l(i):
        return 2 * i

    def slot_of(d, i):
        return slot_r(i) if d == 0 else slot_l(i)

    steps = (half, half - 1)
    edge = (zz, zl)
    toward = (right, left)

    def ag_copy(d, kind, i, at_edge):
        src = x.at[2 * kind, slot_of(d, i - 1)]
        land = 1 - kind if at_edge else kind
        return pltpu.make_async_remote_copy(
            src_ref=src,
            dst_ref=x.at[2 * land, slot_of(d, i)],
            send_sem=ag_send.at[d, kind, i],
            recv_sem=ag_recv.at[d, land, i],
            device_id=toward[d],
            device_id_type=MESH,
        )

    def other_limit(d):
        return edge[d] + 1 if d == 0 else edge[d]

    def ag_own(d, i, act):
        @pl.when(edge[d] <= half - 2)
        def _():
            act(ag_copy(d, 0, i, False))

    def ag_other(d, i, act):
        @pl.when((edge[d] <= half - 2) & (i <= other_limit(d)))
        def _():
            act(ag_copy(d, 1, i, False))

        @pl.when((edge[d] == half - 1) & (i <= other_limit(d)))
        def _():
            act(ag_copy(d, 1, i, True))

    def start(copy):
        copy.start()

    def wait_send(copy):
        copy.wait_send()

    def ag_wait(d, kind, i):
        pltpu.make_async_remote_copy(
            src_ref=x.at[2 * kind, slot_of(d, i)],
            dst_ref=x.at[2 * kind, slot_of(d, i)],
            send_sem=ag_send.at[d, kind, i],
            recv_sem=ag_recv.at[d, kind, i],
            device_id=toward[d],
            device_id_type=MESH,
        ).wait_recv()

    def sib_copy(s):
        return pltpu.make_async_remote_copy(
            src_ref=x.at[0, s],
            dst_ref=x.at[1, s],
            send_sem=sib_send.at[s],
            recv_sem=sib_recv.at[s],
            device_id=sib,
            device_id_type=MESH,
        )

    per_batch = 4 if nz % 4 == 0 else 2
    batches = nz // per_batch
    rows = per_batch * 16

    def stage_one(b):
        lo = b * per_batch
        for s in range(lo, lo + per_batch):
            sib_copy(s).wait_recv()
        xb = x[0:2, lo:lo + per_batch].reshape(2 * rows, feats)
        gate = lax.dot_general(xb, win[0], NT, preferred_element_type=F32)
        up = lax.dot_general(xb, win[1], NT, preferred_element_type=F32)
        grad = lax.dot_general(xb, wdn[...], NT, preferred_element_type=F32)
        gate = gate.reshape(2 * per_batch, 16, hid)[:, 0:8]
        up = up.reshape(2 * per_batch, 16, hid)[:, 0:8]
        grad = grad.reshape(2 * per_batch, 16, hid)[:, 8:16]
        sig = 1.0 / (1.0 + jnp.exp(-gate))
        silu = gate * sig
        hidden = silu * up
        grad_gate = grad * up * (sig * (1.0 + gate * (1.0 - sig)))
        grad_up = grad * silu
        zero = jnp.zeros_like(hidden)
        for k, pair in enumerate(
            ((grad_gate, zero), (grad_up, zero), (zero, hidden))
        ):
            both = jnp.concatenate(pair, axis=1).astype(BF16)
            pre[k, 0:2, lo:lo + per_batch] = both.reshape(2, per_batch, 16, hid)
        for k, pair in enumerate(
            ((zero, grad_gate), (zero, grad_up), (hidden, zero))
        ):
            both = jnp.concatenate(pair, axis=1).astype(BF16)
            pre[3 + k, 0:2, lo:lo + per_batch] = both.reshape(2, per_batch, 16, hid)

    for kind in (1, 0):
        for d in (0, 1):
            (ag_own if kind == 0 else ag_other)(d, 1, start)
    sib_copy(0).start()
    for load in loads[2:]:
        load.wait()
    done = 0
    for i in range(1, half + 1):
        for d in (0, 1):
            if i > steps[d]:
                continue
            ag_wait(d, 0, i)
            if i < steps[d]:
                ag_own(d, i + 1, start)
            sib_copy(slot_of(d, i)).start()

            @pl.when((i <= other_limit(d) - 1) & (i <= steps[d]))
            def _():
                ag_wait(d, 1, i)

            if i < steps[d]:
                ag_other(d, i + 1, start)
        if i < half and 2 * i - 1 >= (done + 1) * per_batch:
            stage_one(done)
            done += 1
    while done < batches:
        stage_one(done)
        done += 1

    def q_copy(b):
        lo = b * per_batch
        return pltpu.make_async_remote_copy(
            src_ref=q.at[pl.ds(lo, per_batch)],
            dst_ref=qr.at[pl.ds(lo, per_batch)],
            send_sem=q_send.at[b],
            recv_sem=q_recv.at[b],
            device_id=sib,
            device_id_type=MESH,
        )

    def stage_two(b):
        lo = b * per_batch
        for c in (1, 0):
            total = None
            for k, w in enumerate((win.at[0], win.at[1], wdn)):
                lhs = pre[3 + k, c, lo:lo + per_batch].reshape(rows, hid)
                term = jnp.dot(lhs, w[...], preferred_element_type=F32)
                total = term if total is None else total + term
            total = total.reshape(per_batch, 16, feats)
            if c == 1:
                q[lo:lo + per_batch] = total.astype(BF16)
                q_copy(b).start()
            else:
                p32[lo:lo + per_batch] = total

    def rs_copy(d, kind, i):
        slot = slot_of(d, i)
        crossing = zz == 0 if d == 0 else zl == 0
        src = sb.at[slot] if kind == 0 else rb.at[d, 1, i]

        def make(land):
            return pltpu.make_async_remote_copy(
                src_ref=src,
                dst_ref=rb.at[d, land, i - 1],
                send_sem=rs_send.at[d, kind, i],
                recv_sem=rs_recv.at[d, land, i - 1],
                device_id=toward[1 - d],
                device_id_type=MESH,
            )

        return crossing, make

    def rs_own(d, i, act):
        crossing, make = rs_copy(d, 0, i)

        @pl.when(crossing)
        def _():
            act(make(1))

        @pl.when(jnp.logical_not(crossing))
        def _():
            act(make(0))

    def rs_other(d, i, act):
        _, make = rs_copy(d, 1, i)

        @pl.when(edge[1 - d] < steps[d] - i)
        def _():
            act(make(1))

    def rs_wait(d, kind, i):
        pltpu.make_async_remote_copy(
            src_ref=rb.at[d, kind, i],
            dst_ref=rb.at[d, kind, i],
            send_sem=rs_send.at[d, kind, i],
            recv_sem=rs_recv.at[d, kind, i],
            device_id=toward[1 - d],
            device_id_type=MESH,
        ).wait_recv()

    def chain(d, i):
        slot = slot_of(d, i)
        if i < steps[d]:
            @pl.when(edge[1 - d] < steps[d] - i)
            def _():
                rs_wait(d, 1, i)

            rs_other(d, i, start)
            has = edge[1 - d] >= 1

            @pl.when(has)
            def _():
                rs_wait(d, 0, i)
                sb[slot] = (
                    p32[slot] + qr[slot].astype(F32) + rb[d, 0, i].astype(F32)
                ).astype(BF16)

            @pl.when(jnp.logical_not(has))
            def _():
                sb[slot] = (p32[slot] + qr[slot].astype(F32)).astype(BF16)
        else:
            sb[slot] = (p32[slot] + qr[slot].astype(F32)).astype(BF16)
        rs_own(d, i, start)

    def g_copy(k):
        peer = lax.rem(dp + k, n_dp)
        return pltpu.make_async_remote_copy(
            src_ref=g.at[peer],
            dst_ref=rg.at[k],
            send_sem=g_send.at[k],
            recv_sem=g_recv.at[k],
            device_id=(peer, ex),
            device_id_type=MESH,
        )

    def g_block(n):
        at = pl.ds(pl.multiple_of(n * 16, 16), 16)
        return jnp.concatenate([g32[kj, at, :] for kj in range(3 * per)], axis=1)

    def weight_grads():
        unit = lax.broadcasted_iota(jnp.int32, (hid, hid), 1)
        row = lax.broadcasted_iota(jnp.int32, (hid, hid), 0)
        want = lax.rem(row, n_dp) * per + lax.div(row, n_dp)
        perm = jnp.where(unit == want, 1.0, 0.0).astype(BF16)
        lhs = jnp.concatenate(
            [
                lax.dot_general(
                    perm, pre[k].reshape(2 * nz * 16, hid), NT, preferred_element_type=F32
                )
                for k in range(3)
            ],
            axis=0,
        ).astype(BF16)
        for r2 in range(blocks // 2):
            xs = x[0:2, :, :, 256 * r2:256 * r2 + 256].reshape(2 * nz * 16, 256)
            term = jnp.dot(lhs, xs, preferred_element_type=F32)
            for r in (0, 1):
                for kj in range(3 * per):
                    g32[kj, pl.ds(2 * r2 + r, n_dp, stride=16), :] = term[
                        kj * n_dp:kj * n_dp + n_dp, 128 * r:128 * r + 128
                    ]

        @pl.loop(1, n_dp)
        def _(k):
            peer = lax.rem(dp + k, n_dp)
            g[peer] = g_block(peer).astype(BF16)
            g_copy(k).start()

    order = list(range(batches - 1, -1, -1))
    stage_two(order[0])
    weight_grads()
    for b in order[1:]:
        stage_two(b)
    arrived = batches
    for j in range(1, half + 1):
        for d in (0, 1):
            i = half + 1 - j if d == 0 else half - j
            if i < 1:
                continue
            while arrived * per_batch > slot_of(d, i):
                arrived -= 1
                q_copy(arrived).wait_recv()
            chain(d, i)
    while arrived > 0:
        arrived -= 1
        q_copy(arrived).wait_recv()

    acc9[...] = g_block(dp)

    @pl.loop(1, n_dp)
    def _(k):
        g_copy(k).wait_recv()
        acc9[...] += rg[k].astype(F32)

    for kj in range(3 * per):
        kind, j = kj // per, kj % per
        for r in range(blocks):
            line = acc9[r:r + 1, kj * 128:kj * 128 + 128]
            if kind < 2:
                gwin_ref[kind, j:j + 1, r * 128:r * 128 + 128] = line
            else:
                gwdn_ref[j:j + 1, r * 128:r * 128 + 128] = line

    p32[0] = p32[0] + qr[0].astype(F32)
    p32[1] = jnp.zeros((16, feats), F32)
    for d in (0, 1):
        @pl.when(edge[1 - d] >= 1)
        def _():
            rs_wait(d, 0, 0)
            p32[0] = p32[0] + rb[d, 0, 0].astype(F32)

        @pl.when(edge[1 - d] < steps[d])
        def _():
            rs_wait(d, 1, 0)
            p32[1] = p32[1] + rb[d, 1, 0].astype(F32)

    mine, theirs = p32[0], p32[1]
    sums = [jnp.where(first, mine, theirs), jnp.where(first, theirs, mine)]
    out_rows = jnp.concatenate([sums[0][0:8], sums[1][0:8]], axis=0) * scale
    grad_rows = jnp.concatenate([sums[0][8:16], sums[1][8:16]], axis=0)
    out_ref[...] = lax.dot_general(
        pick, out_rows.astype(BF16), TN, preferred_element_type=F32
    ).astype(BF16)
    gtok_ref[...] = lax.dot_general(
        pick, grad_rows.astype(BF16), TN, preferred_element_type=F32
    ).astype(BF16)

    for d in (0, 1):
        for i in range(1, steps[d] + 1):
            ag_own(d, i, wait_send)
            ag_other(d, i, wait_send)
            rs_own(d, i, wait_send)
            if i < steps[d]:
                rs_other(d, i, wait_send)
    for s in range(nz):
        sib_copy(s).wait_send()
    for b in range(batches):
        q_copy(b).wait_send()

    @pl.loop(1, n_dp)
    def _(k):
        g_copy(k).wait_send()


def solution(mesh):
    n_dp = mesh.shape["dp"]
    nz = mesh.shape["expert"] // 2

    def step(tokens, expert_ids, gate_weights, cotangent, w_in, w_down):
        ntok, feats = tokens.shape
        hid = w_down.shape[0]
        per = hid // n_dp
        half = nz // 2
        batches = nz // (4 if nz % 4 == 0 else 2)
        vmem = pl.BlockSpec(memory_space=pltpu.VMEM)
        hbm = pl.BlockSpec(memory_space=pl.ANY)
        dma = pltpu.SemaphoreType.DMA
        return pl.pallas_call(
            functools.partial(moe_kernel, n_dp, nz),
            out_shape=(
                jax.ShapeDtypeStruct((ntok, feats), BF16),
                jax.ShapeDtypeStruct((ntok, feats), BF16),
                jax.ShapeDtypeStruct((2, per, feats), F32),
                jax.ShapeDtypeStruct((per, feats), F32),
            ),
            in_specs=[vmem, vmem, hbm, hbm, hbm, hbm],
            out_specs=(vmem, vmem, vmem, vmem),
            scratch_shapes=[
                pltpu.VMEM((ntok, feats), BF16),
                pltpu.VMEM((ntok, feats), BF16),
                pltpu.VMEM((2, hid, feats), BF16),
                pltpu.VMEM((hid, feats), BF16),
                pltpu.VMEM((3, nz, 16, feats), BF16),
                pltpu.VMEM((6, 2, nz, 16, hid), BF16),
                pltpu.VMEM((nz, 16, feats), F32),
                pltpu.VMEM((nz, 16, feats), BF16),
                pltpu.VMEM((nz, 16, feats), BF16),
                pltpu.VMEM((nz, 16, feats), BF16),
                pltpu.VMEM((2, 2, half, 16, feats), BF16),
                pltpu.VMEM((3 * per, n_dp * 16, 128), F32),
                pltpu.VMEM((n_dp, 16, 3 * per * 128), BF16),
                pltpu.VMEM((n_dp, 16, 3 * per * 128), BF16),
                pltpu.VMEM((16, 3 * per * 128), F32),
                dma((4,)),
                dma((2, 2, half + 1)),
                dma((2, 2, half + 1)),
                dma((nz,)),
                dma((nz,)),
                dma((batches,)),
                dma((batches,)),
                dma((2, 2, half + 1)),
                dma((2, 2, half + 1)),
                dma((n_dp,)),
                dma((n_dp,)),
            ],
            compiler_params=pltpu.CompilerParams(
                collective_id=0, has_side_effects=True, vmem_limit_bytes=40 * 2**20
            ),
        )(expert_ids, gate_weights, tokens, cotangent, w_in, w_down)

    in_specs = (
        P(("dp", "expert"), None),
        P(("dp", "expert"), None),
        P(("dp", "expert"), None),
        P(("dp", "expert"), None),
        P(None, "expert", None),
        P("expert", None),
    )
    out_specs = (
        P(("dp", "expert"), None),
        P(("dp", "expert"), None),
        P(None, ("expert", "dp"), None),
        P(("expert", "dp"), None),
    )
    return jax.shard_map(
        step, mesh=mesh, in_specs=in_specs, out_specs=out_specs, check_vma=False
    )
```

```python
import functools

import jax
import jax.numpy as jnp
from jax import lax
from jax.experimental import pallas as pl
from jax.experimental.pallas import tpu as pltpu
from jax.sharding import PartitionSpec as P

MESH = pl.DeviceIdType.MESH
F32 = jnp.float32
BF16 = jnp.bfloat16
NT = (((1,), (1,)), ((), ()))
SPLITS = 2
TN = (((0,), (0,)), ((), ()))


def moe_kernel(
    n_dp, nz,
    ids_ref, gates_ref, tok_hbm, cot_hbm, win_hbm, wdn_hbm,
    rows_ref, pick_ref, acc9,
    tok, cot, win, wdn, x, pre, p32, q, qr, sb, rb, fin, g32, g, rg,
    in_sem, ag_send, ag_recv, far_send, sib_send, sib_recv, q_send, q_recv,
    back_send, rs_recv, fin_recv, g_send, g_recv,
):
    half = nz // 2
    feats = tok.shape[1]
    blocks = feats // 128
    hid = wdn.shape[0]
    per = hid // n_dp
    ntok = tok.shape[0]
    dp = lax.axis_index("dp")
    ex = lax.axis_index("expert")
    z = lax.div(ex, 2)
    core = lax.rem(ex, 2)
    zz = lax.rem(z, half)
    zl = half - 1 - zz
    held = lax.div(z, half)
    sib = (dp, z * 2 + 1 - core)

    loads = [
        pltpu.make_async_copy(tok_hbm, tok, in_sem.at[0]),
        pltpu.make_async_copy(cot_hbm, cot, in_sem.at[1]),
        pltpu.make_async_copy(win_hbm, win, in_sem.at[2]),
        pltpu.make_async_copy(wdn_hbm, wdn, in_sem.at[3]),
    ]
    for load in loads:
        load.start()

    barrier = pltpu.get_barrier_semaphore()
    pl.semaphore_signal(barrier, inc=1, device_id=sib, device_id_type=MESH)

    @pl.loop(1, nz)
    def _(k):
        pl.semaphore_signal(
            barrier, inc=1, device_id=(dp, lax.rem(z + k, nz) * 2 + core), device_id_type=MESH
        )

    @pl.loop(1, n_dp)
    def _(k):
        pl.semaphore_signal(
            barrier, inc=1, device_id=(lax.rem(dp + k, n_dp), ex), device_id_type=MESH
        )

    ids = ids_ref[...]
    gates = gates_ref[...]
    after = lax.broadcasted_iota(jnp.int32, (ntok, ntok), 1)
    before = lax.broadcasted_iota(jnp.int32, (ntok, ntok), 0)
    tri = jnp.where(before < after, 1.0, 0.0).astype(BF16)
    slot = lax.broadcasted_iota(jnp.int32, (8, ntok), 0).astype(F32)
    picks = []
    scales = []
    for e in range(2):
        hit = ids == e
        chosen = jnp.max(jnp.where(hit, 1.0, 0.0), axis=0, keepdims=True)
        weight = jnp.sum(jnp.where(hit, gates, 0.0), axis=0, keepdims=True)
        chosen = jnp.broadcast_to(chosen, (8, ntok))
        rank = jnp.dot(
            jnp.concatenate([chosen, chosen], axis=0).astype(BF16), tri,
            preferred_element_type=F32,
        )[0:8]
        pick = jnp.where((chosen > 0.5) & (rank == slot), 1.0, 0.0)
        picks.append(pick)
        scales.append(jnp.sum(pick * weight, axis=1, keepdims=True))
    pick = jnp.concatenate(picks, axis=0).astype(BF16)
    scale = jnp.concatenate(scales, axis=0)

    loads[0].wait()
    tok_rows = jnp.dot(pick, tok[...], preferred_element_type=F32)
    loads[1].wait()
    cot_rows = jnp.dot(pick, cot[...], preferred_element_type=F32) * scale
    packet = [
        jnp.concatenate([tok_rows[8 * e:8 * e + 8], cot_rows[8 * e:8 * e + 8]], axis=0)
        for e in range(2)
    ]
    first = held == 0
    x[0, 0] = jnp.where(first, packet[0], packet[1]).astype(BF16)
    x[0, nz] = jnp.where(first, packet[1], packet[0]).astype(BF16)

    pl.semaphore_wait(barrier, nz + n_dp - 1)

    def slot_of(d, i):
        return 0 if i == 0 else (2 * i - 1 if d == 0 else 2 * i)

    steps = (half, half - 1)
    edge = (zz, zl)
    wide = feats // SPLITS

    def cols(h):
        return pl.ds(h * wide, wide)

    def away(d, i):
        return (dp, lax.rem(z + (i if d == 0 else nz - i), nz) * 2 + core)

    def remote(src, dst, send, recv, dev):
        return pltpu.make_async_remote_copy(
            src_ref=src, dst_ref=dst, send_sem=send, recv_sem=recv,
            device_id=dev, device_id_type=MESH,
        )

    def start(copy):
        copy.start()

    def wait_send(copy):
        copy.wait_send()

    def passes(d):
        return edge[d] <= half - 2

    def ag_chain(d, i, h, act):
        @pl.when(passes(d))
        def _():
            act(remote(
                x.at[0, slot_of(d, i), :, cols(h)], x.at[0, slot_of(d, i + 1), :, cols(h)],
                ag_send.at[d, i, h], ag_recv.at[d, i + 1, h], away(d, 1),
            ))

    def ag_direct(d, i, h):
        at = 2 * i - 1 if d == 0 else 2 * i
        return remote(
            x.at[0, nz, :, cols(h)], x.at[0, at, :, cols(h)],
            far_send.at[d, h], ag_recv.at[d, i, h], away(d, i),
        )

    def ag_export(d, h, act):
        dist = half - edge[d]

        @pl.when(dist <= steps[d])
        def _():
            act(ag_direct(d, dist, h))

    def ag_wait(d, i, h):
        at = x.at[0, slot_of(d, i), :, cols(h)]
        remote(at, at, ag_send.at[d, i, h], ag_recv.at[d, i, h], away(d, 1)).wait_recv()

    def sib_copy(s):
        return remote(x.at[0, s], x.at[1, s], sib_send.at[s], sib_recv.at[s], sib)

    per_batch = 4 if nz % 4 == 0 else 2
    batches = nz // per_batch
    rows = per_batch * 16

    def stage_one(b):
        lo = b * per_batch
        for s in range(lo, lo + per_batch):
            sib_copy(s).wait_recv()
        xb = x[0:2, lo:lo + per_batch].reshape(2 * rows, feats)
        gate = lax.dot_general(xb, win[0], NT, preferred_element_type=F32)
        up = lax.dot_general(xb, win[1], NT, preferred_element_type=F32)
        grad = lax.dot_general(xb, wdn[...], NT, preferred_element_type=F32)
        gate = gate.reshape(2 * per_batch, 16, hid)[:, 0:8]
        up = up.reshape(2 * per_batch, 16, hid)[:, 0:8]
        grad = grad.reshape(2 * per_batch, 16, hid)[:, 8:16]
        sig = 1.0 / (1.0 + jnp.exp(-gate))
        silu = gate * sig
        hidden = silu * up
        grad_gate = grad * up * (sig * (1.0 + gate * (1.0 - sig)))
        grad_up = grad * silu
        zero = jnp.zeros_like(hidden)
        for k, pair in enumerate(
            ((grad_gate, zero), (grad_up, zero), (zero, hidden))
        ):
            both = jnp.concatenate(pair, axis=1).astype(BF16)
            pre[k, 0:2, lo:lo + per_batch] = both.reshape(2, per_batch, 16, hid)
        for k, pair in enumerate(
            ((zero, grad_gate), (zero, grad_up), (hidden, zero))
        ):
            both = jnp.concatenate(pair, axis=1).astype(BF16)
            pre[3 + k, 0:2, lo:lo + per_batch] = both.reshape(2, per_batch, 16, hid)

    for h in range(SPLITS):
        for d in (0, 1):
            ag_chain(d, 0, h, start)

    def export_at(d, when):
        @pl.when(when)
        def _():
            for h in range(SPLITS):
                ag_export(d, h, start)

    for d in (0, 1):
        export_at(d, edge[d] >= half - 2)
    sib_copy(0).start()
    for load in loads[2:]:
        load.wait()
    done = 0
    for i in range(1, half + 1):
        for h in range(SPLITS):
            for d in (0, 1):
                if i <= steps[d]:
                    ag_wait(d, i, h)
                    if i < steps[d]:
                        ag_chain(d, i, h, start)
        for d in (0, 1):
            if 2 * i < half:
                export_at(
                    d, (edge[d] < half - 2 * i) & (edge[d] >= half - 2 - 2 * i)
                )
        for d in (0, 1):
            if i <= steps[d]:
                sib_copy(slot_of(d, i)).start()
        if i < half and 2 * i - 1 >= (done + 1) * per_batch:
            stage_one(done)
            done += 1
    while done < batches:
        stage_one(done)
        done += 1

    def q_copy(b):
        at = pl.ds(b * per_batch, per_batch)
        return remote(q.at[at], qr.at[at], q_send.at[b], q_recv.at[b], sib)

    def stage_two(b):
        lo = b * per_batch
        for c in (1, 0):
            total = None
            for k, w in enumerate((win.at[0], win.at[1], wdn)):
                lhs = pre[3 + k, c, lo:lo + per_batch].reshape(rows, hid)
                term = jnp.dot(lhs, w[...], preferred_element_type=F32)
                total = term if total is None else total + term
            total = total.reshape(per_batch, 16, feats)
            if c == 1:
                q[lo:lo + per_batch] = total.astype(BF16)
                q_copy(b).start()
            else:
                p32[lo:lo + per_batch] = total

    def rs_send(d, i, h, act):
        src = sb.at[slot_of(d, i), :, cols(h)]
        def final(kind):
            return remote(
                src, fin.at[d, kind, :, cols(h)],
                back_send.at[d, i, h], fin_recv.at[d, kind, h], away(1 - d, i),
            )

        @pl.when(edge[d] == 0)
        def _():
            act(final(1))

        @pl.when(edge[d] != 0)
        def _():
            if i == 1:
                act(final(0))
            else:
                act(remote(
                    src, rb.at[d, i - 1, :, cols(h)],
                    back_send.at[d, i, h], rs_recv.at[d, i - 1, h], away(1 - d, 1),
                ))

    def chain(d, i, h):
        slot = slot_of(d, i)
        at = cols(h)
        if i < steps[d]:
            has = passes(d)

            @pl.when(has)
            def _():
                here = rb.at[d, i, :, at]
                remote(
                    here, here, back_send.at[d, i, h], rs_recv.at[d, i, h], away(1 - d, 1)
                ).wait_recv()
                sb[slot, :, at] = (p32[slot, :, at] + rb[d, i, :, at].astype(F32)).astype(BF16)

            @pl.when(jnp.logical_not(has))
            def _():
                sb[slot, :, at] = p32[slot, :, at].astype(BF16)
        else:
            sb[slot, :, at] = p32[slot, :, at].astype(BF16)
        rs_send(d, i, h, start)

    def g_copy(k):
        peer = lax.rem(dp + k, n_dp)
        return pltpu.make_async_remote_copy(
            src_ref=g.at[peer],
            dst_ref=rg.at[k],
            send_sem=g_send.at[k],
            recv_sem=g_recv.at[k],
            device_id=(peer, ex),
            device_id_type=MESH,
        )

    def g_block(n):
        at = pl.ds(pl.multiple_of(n * 16, 16), 16)
        return jnp.concatenate([g32[kj, at, :] for kj in range(3 * per)], axis=1)

    def weight_grads():
        unit = lax.broadcasted_iota(jnp.int32, (hid, hid), 1)
        row = lax.broadcasted_iota(jnp.int32, (hid, hid), 0)
        want = lax.rem(row, n_dp) * per + lax.div(row, n_dp)
        perm = jnp.where(unit == want, 1.0, 0.0).astype(BF16)
        lhs = jnp.concatenate(
            [
                lax.dot_general(
                    perm, pre[k].reshape(2 * nz * 16, hid), NT, preferred_element_type=F32
                )
                for k in range(3)
            ],
            axis=0,
        ).astype(BF16)
        for r2 in range(blocks // 2):
            xs = x[0:2, 0:nz, :, 256 * r2:256 * r2 + 256].reshape(2 * nz * 16, 256)
            term = jnp.dot(lhs, xs, preferred_element_type=F32)
            for r in (0, 1):
                for kj in range(3 * per):
                    g32[kj, pl.ds(2 * r2 + r, n_dp, stride=16), :] = term[
                        kj * n_dp:kj * n_dp + n_dp, 128 * r:128 * r + 128
                    ]

        @pl.loop(1, n_dp)
        def _(k):
            peer = lax.rem(dp + k, n_dp)
            g[peer] = g_block(peer).astype(BF16)
            g_copy(k).start()

    pending = list(range(batches - 1, -1, -1))
    arrived = batches

    def next_stage():
        if pending:
            stage_two(pending.pop(0))

    next_stage()
    next_stage()
    for j in range(1, half + 1):
        hops = [(d, (half + 1 if d == 0 else half) - j) for d in (0, 1)]
        hops = [(d, i) for d, i in hops if i >= 1]
        low = min(slot_of(d, i) for d, i in hops)
        while arrived * per_batch > low:
            arrived -= 1
            if arrived in pending:
                next_stage()
            q_copy(arrived).wait_recv()
            at = pl.ds(arrived * per_batch, per_batch)
            p32[at] = p32[at] + qr[at].astype(F32)
        for h in range(SPLITS):
            for d, i in hops:
                chain(d, i, h)
        if j == 1:
            weight_grads()
        else:
            next_stage()
    while arrived > 0:
        arrived -= 1
        q_copy(arrived).wait_recv()
        at = pl.ds(arrived * per_batch, per_batch)
        p32[at] = p32[at] + qr[at].astype(F32)

    acc9[...] = g_block(dp)

    @pl.loop(1, n_dp)
    def _(k):
        g_copy(k).wait_recv()
        acc9[...] += rg[k].astype(F32)

    p32[1] = jnp.zeros((16, feats), F32)

    def take(d, kind):
        for h in range(SPLITS):
            here = fin.at[d, kind, :, cols(h)]
            remote(
                here, here, back_send.at[d, 1, h], fin_recv.at[d, kind, h], away(1 - d, 1)
            ).wait_recv()
        p32[kind] = p32[kind] + fin[d, kind].astype(F32)

    for d in (0, 1):
        pl.when(half - edge[d] <= steps[d])(functools.partial(take, d, 1))
        pl.when(edge[d] <= half - 2)(functools.partial(take, d, 0))

    mine, theirs = p32[0], p32[1]
    sums = [jnp.where(first, mine, theirs), jnp.where(first, theirs, mine)]
    out_rows = jnp.concatenate([sums[0][0:8], sums[1][0:8]], axis=0) * scale
    grad_rows = jnp.concatenate([sums[0][8:16], sums[1][8:16]], axis=0)
    rows_ref[0:16] = out_rows.astype(BF16)
    rows_ref[16:32] = grad_rows.astype(BF16)
    pick_ref[...] = pick

    for h in range(SPLITS):
        for d in (0, 1):
            ag_export(d, h, wait_send)
            for i in range(steps[d]):
                ag_chain(d, i, h, wait_send)
                rs_send(d, i + 1, h, wait_send)
    for s in range(nz):
        sib_copy(s).wait_send()
    for b in range(batches):
        q_copy(b).wait_send()

    @pl.loop(1, n_dp)
    def _(k):
        g_copy(k).wait_send()


def place_kernel(rows_ref, pick_ref, acc9, out_ref, gtok_ref, gwin_ref, gwdn_ref):
    pick = pick_ref[...]
    for ref, rows in ((out_ref, rows_ref[0:16]), (gtok_ref, rows_ref[16:32])):
        ref[...] = lax.dot_general(pick, rows, TN, preferred_element_type=F32).astype(BF16)
    per = gwdn_ref.shape[0]
    for kj in range(3 * per):
        kind, j = kj // per, kj % per
        for r in range(16):
            line = acc9[r:r + 1, kj * 128:kj * 128 + 128]
            if kind < 2:
                gwin_ref[j, kind:kind + 1, r * 128:r * 128 + 128] = line
            else:
                gwdn_ref[j:j + 1, r * 128:r * 128 + 128] = line


def solution(mesh):
    n_dp = mesh.shape["dp"]
    nz = mesh.shape["expert"] // 2

    def step(tokens, expert_ids, gate_weights, cotangent, w_in, w_down):
        ntok, feats = tokens.shape
        hid = w_down.shape[0]
        per = hid // n_dp
        half = nz // 2
        batches = nz // (4 if nz % 4 == 0 else 2)
        vmem = pl.BlockSpec(memory_space=pltpu.VMEM)
        hbm = pl.BlockSpec(memory_space=pl.ANY)
        dma = pltpu.SemaphoreType.DMA
        rows, pick, sums = pl.pallas_call(
            functools.partial(moe_kernel, n_dp, nz),
            out_shape=(
                jax.ShapeDtypeStruct((32, feats), BF16),
                jax.ShapeDtypeStruct((16, ntok), BF16),
                jax.ShapeDtypeStruct((16, 3 * per * 128), F32),
            ),
            in_specs=[vmem, vmem, hbm, hbm, hbm, hbm],
            out_specs=(vmem, vmem, vmem),
            scratch_shapes=[
                pltpu.VMEM((ntok, feats), BF16),
                pltpu.VMEM((ntok, feats), BF16),
                pltpu.VMEM((2, hid, feats), BF16),
                pltpu.VMEM((hid, feats), BF16),
                pltpu.VMEM((2, nz + 1, 16, feats), BF16),
                pltpu.VMEM((6, 2, nz, 16, hid), BF16),
                pltpu.VMEM((nz, 16, feats), F32),
                pltpu.VMEM((nz, 16, feats), BF16),
                pltpu.VMEM((nz, 16, feats), BF16),
                pltpu.VMEM((nz, 16, feats), BF16),
                pltpu.VMEM((2, half, 16, feats), BF16),
                pltpu.VMEM((2, 2, 16, feats), BF16),
                pltpu.VMEM((3 * per, n_dp * 16, 128), F32),
                pltpu.VMEM((n_dp, 16, 3 * per * 128), BF16),
                pltpu.VMEM((n_dp, 16, 3 * per * 128), BF16),
                dma((4,)),
                dma((2, half, SPLITS)),
                dma((2, half + 1, SPLITS)),
                dma((2, SPLITS)),
                dma((nz,)),
                dma((nz,)),
                dma((batches,)),
                dma((batches,)),
                dma((2, half + 1, SPLITS)),
                dma((2, half, SPLITS)),
                dma((2, 2, SPLITS)),
                dma((n_dp,)),
                dma((n_dp,)),
            ],
            compiler_params=pltpu.CompilerParams(
                collective_id=0, has_side_effects=True, vmem_limit_bytes=62 * 2**20
            ),
        )(expert_ids.T, gate_weights.T, tokens, cotangent, w_in, w_down)
        out, grad, grad_in, grad_down = pl.pallas_call(
            place_kernel,
            out_shape=(
                jax.ShapeDtypeStruct((ntok, feats), BF16),
                jax.ShapeDtypeStruct((ntok, feats), BF16),
                jax.ShapeDtypeStruct((per, 2, feats), F32),
                jax.ShapeDtypeStruct((per, feats), F32),
            ),
            in_specs=[vmem, vmem, vmem],
            out_specs=(vmem, vmem, vmem, vmem),
        )(rows, pick, sums)
        return out, grad, jnp.transpose(grad_in, (1, 0, 2)), grad_down

    in_specs = (
        P(("dp", "expert"), None),
        P(("dp", "expert"), None),
        P(("dp", "expert"), None),
        P(("dp", "expert"), None),
        P(None, "expert", None),
        P("expert", None),
    )
    out_specs = (
        P(("dp", "expert"), None),
        P(("dp", "expert"), None),
        P(None, ("expert", "dp"), None),
        P(("expert", "dp"), None),
    )
    return jax.shard_map(
        step, mesh=mesh, in_specs=in_specs, out_specs=out_specs, check_vma=False
    )
```

```python
import functools

import jax
import jax.numpy as jnp
from jax import lax
from jax.experimental import pallas as pl
from jax.experimental.pallas import tpu as pltpu
from jax.sharding import PartitionSpec as P

MESH = pl.DeviceIdType.MESH
F32 = jnp.float32
BF16 = jnp.bfloat16
NT = (((1,), (1,)), ((), ()))
SPLITS = 2
TN = (((0,), (0,)), ((), ()))


def moe_kernel(
    n_dp, nz,
    ids_ref, gates_ref, tok_hbm, cot_hbm, win_hbm, wdn_hbm,
    rows_ref, pick_ref, acc9,
    tok, cot, win, wdn, x, pre, p32, q, qr, sb, rb, fin, g32, g, rg,
    in_sem, ag_send, ag_recv, far_send, sib_send, sib_recv, q_send, q_recv,
    back_send, rs_recv, fin_recv, g_send, g_recv,
):
    half = nz // 2
    feats = tok.shape[1]
    blocks = feats // 128
    hid = wdn.shape[0]
    per = hid // n_dp
    ntok = tok.shape[0]
    dp = lax.axis_index("dp")
    ex = lax.axis_index("expert")
    z = lax.div(ex, 2)
    core = lax.rem(ex, 2)
    zz = lax.rem(z, half)
    zl = half - 1 - zz
    held = lax.div(z, half)
    sib = (dp, z * 2 + 1 - core)

    loads = [
        pltpu.make_async_copy(tok_hbm, tok, in_sem.at[0]),
        pltpu.make_async_copy(cot_hbm, cot, in_sem.at[1]),
        pltpu.make_async_copy(win_hbm, win, in_sem.at[2]),
        pltpu.make_async_copy(wdn_hbm, wdn, in_sem.at[3]),
    ]
    for load in loads:
        load.start()

    barrier = pltpu.get_barrier_semaphore()
    pl.semaphore_signal(barrier, inc=1, device_id=sib, device_id_type=MESH)

    @pl.loop(1, nz)
    def _(k):
        pl.semaphore_signal(
            barrier, inc=1, device_id=(dp, lax.rem(z + k, nz) * 2 + core), device_id_type=MESH
        )

    @pl.loop(1, n_dp)
    def _(k):
        pl.semaphore_signal(
            barrier, inc=1, device_id=(lax.rem(dp + k, n_dp), ex), device_id_type=MESH
        )

    ids = ids_ref[...]
    gates = gates_ref[...]
    after = lax.broadcasted_iota(jnp.int32, (ntok, ntok), 1)
    before = lax.broadcasted_iota(jnp.int32, (ntok, ntok), 0)
    tri = jnp.where(before < after, 1.0, 0.0).astype(BF16)
    slot = lax.broadcasted_iota(jnp.int32, (8, ntok), 0).astype(F32)
    picks = []
    scales = []
    for e in range(2):
        hit = ids == e
        chosen = jnp.max(jnp.where(hit, 1.0, 0.0), axis=0, keepdims=True)
        weight = jnp.sum(jnp.where(hit, gates, 0.0), axis=0, keepdims=True)
        chosen = jnp.broadcast_to(chosen, (8, ntok))
        rank = jnp.dot(
            jnp.concatenate([chosen, chosen], axis=0).astype(BF16), tri,
            preferred_element_type=F32,
        )[0:8]
        pick = jnp.where((chosen > 0.5) & (rank == slot), 1.0, 0.0)
        picks.append(pick)
        scales.append(jnp.sum(pick * weight, axis=1, keepdims=True))
    pick = jnp.concatenate(picks, axis=0).astype(BF16)
    scale = jnp.concatenate(scales, axis=0)

    loads[0].wait()
    tok_rows = jnp.dot(pick, tok[...], preferred_element_type=F32)
    loads[1].wait()
    cot_rows = jnp.dot(pick, cot[...], preferred_element_type=F32) * scale
    packet = [
        jnp.concatenate([tok_rows[8 * e:8 * e + 8], cot_rows[8 * e:8 * e + 8]], axis=0)
        for e in range(2)
    ]
    first = held == 0
    x[0, 0] = jnp.where(first, packet[0], packet[1]).astype(BF16)
    x[0, nz] = jnp.where(first, packet[1], packet[0]).astype(BF16)

    pl.semaphore_wait(barrier, nz + n_dp - 1)

    def slot_of(d, i):
        return 0 if i == 0 else (2 * i - 1 if d == 0 else 2 * i)

    steps = (half, half - 1)
    edge = (zz, zl)
    wide = feats // SPLITS

    def cols(h):
        return pl.ds(h * wide, wide)

    def away(d, i):
        return (dp, lax.rem(z + (i if d == 0 else nz - i), nz) * 2 + core)

    def remote(src, dst, send, recv, dev):
        return pltpu.make_async_remote_copy(
            src_ref=src, dst_ref=dst, send_sem=send, recv_sem=recv,
            device_id=dev, device_id_type=MESH,
        )

    def start(copy):
        copy.start()

    def wait_send(copy):
        copy.wait_send()

    def passes(d):
        return edge[d] <= half - 2

    def ag_chain(d, i, h, act):
        @pl.when(passes(d))
        def _():
            act(remote(
                x.at[0, slot_of(d, i), :, cols(h)], x.at[0, slot_of(d, i + 1), :, cols(h)],
                ag_send.at[d, i, h], ag_recv.at[d, i + 1, h], away(d, 1),
            ))

    def ag_direct(d, i, h):
        at = 2 * i - 1 if d == 0 else 2 * i
        return remote(
            x.at[0, nz, :, cols(h)], x.at[0, at, :, cols(h)],
            far_send.at[d, h], ag_recv.at[d, i, h], away(d, i),
        )

    def ag_export(d, h, act):
        dist = half - edge[d]

        @pl.when(dist <= steps[d])
        def _():
            act(ag_direct(d, dist, h))

    def ag_wait(d, i, h):
        at = x.at[0, slot_of(d, i), :, cols(h)]
        remote(at, at, ag_send.at[d, i, h], ag_recv.at[d, i, h], away(d, 1)).wait_recv()

    def sib_copy(s):
        return remote(x.at[0, s], x.at[1, s], sib_send.at[s], sib_recv.at[s], sib)

    per_batch = 2
    batches = nz // per_batch
    rows = per_batch * 16

    def stage_one(b):
        lo = b * per_batch
        for s in range(lo, lo + per_batch):
            sib_copy(s).wait_recv()
        xb = x[0:2, lo:lo + per_batch].reshape(2 * rows, feats)
        gate = lax.dot_general(xb, win[0], NT, preferred_element_type=F32)
        up = lax.dot_general(xb, win[1], NT, preferred_element_type=F32)
        grad = lax.dot_general(xb, wdn[...], NT, preferred_element_type=F32)
        gate = gate.reshape(2 * per_batch, 16, hid)[:, 0:8]
        up = up.reshape(2 * per_batch, 16, hid)[:, 0:8]
        grad = grad.reshape(2 * per_batch, 16, hid)[:, 8:16]
        sig = 1.0 / (1.0 + jnp.exp(-gate))
        silu = gate * sig
        hidden = silu * up
        grad_gate = grad * up * (sig * (1.0 + gate * (1.0 - sig)))
        grad_up = grad * silu
        zero = jnp.zeros_like(hidden)
        for k, pair in enumerate(
            ((grad_gate, zero), (grad_up, zero), (zero, hidden))
        ):
            both = jnp.concatenate(pair, axis=1).astype(BF16)
            pre[k, 0:2, lo:lo + per_batch] = both.reshape(2, per_batch, 16, hid)
        for k, pair in enumerate(
            ((zero, grad_gate), (zero, grad_up), (hidden, zero))
        ):
            both = jnp.concatenate(pair, axis=1).astype(BF16)
            pre[3 + k, 0:2, lo:lo + per_batch] = both.reshape(2, per_batch, 16, hid)

    for h in range(SPLITS):
        for d in (0, 1):
            ag_chain(d, 0, h, start)

    def export_at(d, when):
        @pl.when(when)
        def _():
            for h in range(SPLITS):
                ag_export(d, h, start)

    for d in (0, 1):
        export_at(d, edge[d] >= half - 2)
    sib_copy(0).start()
    for load in loads[2:]:
        load.wait()
    done = 0
    for i in range(1, half + 1):
        for h in range(SPLITS):
            for d in (0, 1):
                if i <= steps[d]:
                    ag_wait(d, i, h)
                    if i < steps[d]:
                        ag_chain(d, i, h, start)
        for d in (0, 1):
            if 2 * i < half:
                export_at(
                    d, (edge[d] < half - 2 * i) & (edge[d] >= half - 2 - 2 * i)
                )
        for d in (0, 1):
            if i <= steps[d]:
                sib_copy(slot_of(d, i)).start()
        if i < half and 2 * i - 1 >= (done + 1) * per_batch:
            stage_one(done)
            done += 1
    while done < batches:
        stage_one(done)
        done += 1

    def q_copy(b):
        at = pl.ds(b * per_batch, per_batch)
        return remote(q.at[at], qr.at[at], q_send.at[b], q_recv.at[b], sib)

    def stage_two(b):
        lo = b * per_batch
        for c in (1, 0):
            total = None
            for k, w in enumerate((win.at[0], win.at[1], wdn)):
                lhs = pre[3 + k, c, lo:lo + per_batch].reshape(rows, hid)
                term = jnp.dot(lhs, w[...], preferred_element_type=F32)
                total = term if total is None else total + term
            total = total.reshape(per_batch, 16, feats)
            if c == 1:
                q[lo:lo + per_batch] = total.astype(BF16)
                q_copy(b).start()
            else:
                p32[lo:lo + per_batch] = total

    def rs_send(d, i, h, act):
        src = sb.at[slot_of(d, i), :, cols(h)]
        def final(kind):
            return remote(
                src, fin.at[d, kind, :, cols(h)],
                back_send.at[d, i, h], fin_recv.at[d, kind, h], away(1 - d, i),
            )

        @pl.when(edge[d] == 0)
        def _():
            act(final(1))

        @pl.when(edge[d] != 0)
        def _():
            if i == 1:
                act(final(0))
            else:
                act(remote(
                    src, rb.at[d, i - 1, :, cols(h)],
                    back_send.at[d, i, h], rs_recv.at[d, i - 1, h], away(1 - d, 1),
                ))

    def chain(d, i, h):
        slot = slot_of(d, i)
        at = cols(h)
        if i < steps[d]:
            has = passes(d)

            @pl.when(has)
            def _():
                here = rb.at[d, i, :, at]
                remote(
                    here, here, back_send.at[d, i, h], rs_recv.at[d, i, h], away(1 - d, 1)
                ).wait_recv()
                sb[slot, :, at] = (p32[slot, :, at] + rb[d, i, :, at].astype(F32)).astype(BF16)

            @pl.when(jnp.logical_not(has))
            def _():
                sb[slot, :, at] = p32[slot, :, at].astype(BF16)
        else:
            sb[slot, :, at] = p32[slot, :, at].astype(BF16)
        rs_send(d, i, h, start)

    def g_copy(k):
        peer = lax.rem(dp + k, n_dp)
        return pltpu.make_async_remote_copy(
            src_ref=g.at[peer],
            dst_ref=rg.at[k],
            send_sem=g_send.at[k],
            recv_sem=g_recv.at[k],
            device_id=(peer, ex),
            device_id_type=MESH,
        )

    def g_block(n):
        at = pl.ds(pl.multiple_of(n * 16, 16), 16)
        return jnp.concatenate([g32[kj, at, :] for kj in range(3 * per)], axis=1)

    def weight_grads():
        unit = lax.broadcasted_iota(jnp.int32, (hid, hid), 1)
        row = lax.broadcasted_iota(jnp.int32, (hid, hid), 0)
        want = lax.rem(row, n_dp) * per + lax.div(row, n_dp)
        perm = jnp.where(unit == want, 1.0, 0.0).astype(BF16)
        lhs = jnp.concatenate(
            [
                lax.dot_general(
                    perm, pre[k].reshape(2 * nz * 16, hid), NT, preferred_element_type=F32
                )
                for k in range(3)
            ],
            axis=0,
        ).astype(BF16)
        for r2 in range(blocks // 2):
            xs = x[0:2, 0:nz, :, 256 * r2:256 * r2 + 256].reshape(2 * nz * 16, 256)
            term = jnp.dot(lhs, xs, preferred_element_type=F32)
            for r in (0, 1):
                for kj in range(3 * per):
                    g32[kj, pl.ds(2 * r2 + r, n_dp, stride=16), :] = term[
                        kj * n_dp:kj * n_dp + n_dp, 128 * r:128 * r + 128
                    ]

        @pl.loop(1, n_dp)
        def _(k):
            peer = lax.rem(dp + k, n_dp)
            g[peer] = g_block(peer).astype(BF16)
            g_copy(k).start()

    pending = list(range(batches - 1, -1, -1))
    arrived = batches

    def next_stage():
        if pending:
            stage_two(pending.pop(0))

    next_stage()
    next_stage()
    for j in range(1, half + 1):
        hops = [(d, (half + 1 if d == 0 else half) - j) for d in (0, 1)]
        hops = [(d, i) for d, i in hops if i >= 1]
        low = min(slot_of(d, i) for d, i in hops)
        while arrived * per_batch > low:
            arrived -= 1
            if arrived in pending:
                next_stage()
            q_copy(arrived).wait_recv()
            at = pl.ds(arrived * per_batch, per_batch)
            p32[at] = p32[at] + qr[at].astype(F32)
        for h in range(SPLITS):
            for d, i in hops:
                chain(d, i, h)
        if j == 1:
            weight_grads()
        else:
            next_stage()
    while arrived > 0:
        arrived -= 1
        q_copy(arrived).wait_recv()
        at = pl.ds(arrived * per_batch, per_batch)
        p32[at] = p32[at] + qr[at].astype(F32)

    acc9[...] = g_block(dp)

    @pl.loop(1, n_dp)
    def _(k):
        g_copy(k).wait_recv()
        acc9[...] += rg[k].astype(F32)

    p32[1] = jnp.zeros((16, feats), F32)

    def take(d, kind):
        for h in range(SPLITS):
            here = fin.at[d, kind, :, cols(h)]
            remote(
                here, here, back_send.at[d, 1, h], fin_recv.at[d, kind, h], away(1 - d, 1)
            ).wait_recv()
        p32[kind] = p32[kind] + fin[d, kind].astype(F32)

    for d in (0, 1):
        pl.when(half - edge[d] <= steps[d])(functools.partial(take, d, 1))
        pl.when(edge[d] <= half - 2)(functools.partial(take, d, 0))

    mine, theirs = p32[0], p32[1]
    sums = [jnp.where(first, mine, theirs), jnp.where(first, theirs, mine)]
    out_rows = jnp.concatenate([sums[0][0:8], sums[1][0:8]], axis=0) * scale
    grad_rows = jnp.concatenate([sums[0][8:16], sums[1][8:16]], axis=0)
    rows_ref[0:16] = out_rows.astype(BF16)
    rows_ref[16:32] = grad_rows.astype(BF16)
    pick_ref[...] = pick

    for h in range(SPLITS):
        for d in (0, 1):
            ag_export(d, h, wait_send)
            for i in range(steps[d]):
                ag_chain(d, i, h, wait_send)
                rs_send(d, i + 1, h, wait_send)
    for s in range(nz):
        sib_copy(s).wait_send()
    for b in range(batches):
        q_copy(b).wait_send()

    @pl.loop(1, n_dp)
    def _(k):
        g_copy(k).wait_send()


def place_kernel(rows_ref, pick_ref, acc9, out_ref, gtok_ref, gwin_ref, gwdn_ref):
    pick = pick_ref[...]
    for ref, rows in ((out_ref, rows_ref[0:16]), (gtok_ref, rows_ref[16:32])):
        ref[...] = lax.dot_general(pick, rows, TN, preferred_element_type=F32).astype(BF16)
    per = gwdn_ref.shape[0]
    for kj in range(3 * per):
        kind, j = kj // per, kj % per
        for r in range(16):
            line = acc9[r:r + 1, kj * 128:kj * 128 + 128]
            if kind < 2:
                gwin_ref[j, kind:kind + 1, r * 128:r * 128 + 128] = line
            else:
                gwdn_ref[j:j + 1, r * 128:r * 128 + 128] = line


def solution(mesh):
    n_dp = mesh.shape["dp"]
    nz = mesh.shape["expert"] // 2

    def step(tokens, expert_ids, gate_weights, cotangent, w_in, w_down):
        ntok, feats = tokens.shape
        hid = w_down.shape[0]
        per = hid // n_dp
        half = nz // 2
        batches = nz // 2
        vmem = pl.BlockSpec(memory_space=pltpu.VMEM)
        hbm = pl.BlockSpec(memory_space=pl.ANY)
        dma = pltpu.SemaphoreType.DMA
        rows, pick, sums = pl.pallas_call(
            functools.partial(moe_kernel, n_dp, nz),
            out_shape=(
                jax.ShapeDtypeStruct((32, feats), BF16),
                jax.ShapeDtypeStruct((16, ntok), BF16),
                jax.ShapeDtypeStruct((16, 3 * per * 128), F32),
            ),
            in_specs=[vmem, vmem, hbm, hbm, hbm, hbm],
            out_specs=(vmem, vmem, vmem),
            scratch_shapes=[
                pltpu.VMEM((ntok, feats), BF16),
                pltpu.VMEM((ntok, feats), BF16),
                pltpu.VMEM((2, hid, feats), BF16),
                pltpu.VMEM((hid, feats), BF16),
                pltpu.VMEM((2, nz + 1, 16, feats), BF16),
                pltpu.VMEM((6, 2, nz, 16, hid), BF16),
                pltpu.VMEM((nz, 16, feats), F32),
                pltpu.VMEM((nz, 16, feats), BF16),
                pltpu.VMEM((nz, 16, feats), BF16),
                pltpu.VMEM((nz, 16, feats), BF16),
                pltpu.VMEM((2, half, 16, feats), BF16),
                pltpu.VMEM((2, 2, 16, feats), BF16),
                pltpu.VMEM((3 * per, n_dp * 16, 128), F32),
                pltpu.VMEM((n_dp, 16, 3 * per * 128), BF16),
                pltpu.VMEM((n_dp, 16, 3 * per * 128), BF16),
                dma((4,)),
                dma((2, half, SPLITS)),
                dma((2, half + 1, SPLITS)),
                dma((2, SPLITS)),
                dma((nz,)),
                dma((nz,)),
                dma((batches,)),
                dma((batches,)),
                dma((2, half + 1, SPLITS)),
                dma((2, half, SPLITS)),
                dma((2, 2, SPLITS)),
                dma((n_dp,)),
                dma((n_dp,)),
            ],
            compiler_params=pltpu.CompilerParams(
                collective_id=0, has_side_effects=True, vmem_limit_bytes=62 * 2**20
            ),
        )(expert_ids.T, gate_weights.T, tokens, cotangent, w_in, w_down)
        out, grad, grad_in, grad_down = pl.pallas_call(
            place_kernel,
            out_shape=(
                jax.ShapeDtypeStruct((ntok, feats), BF16),
                jax.ShapeDtypeStruct((ntok, feats), BF16),
                jax.ShapeDtypeStruct((per, 2, feats), F32),
                jax.ShapeDtypeStruct((per, feats), F32),
            ),
            in_specs=[vmem, vmem, vmem],
            out_specs=(vmem, vmem, vmem, vmem),
        )(rows, pick, sums)
        return out, grad, jnp.transpose(grad_in, (1, 0, 2)), grad_down

    in_specs = (
        P(("dp", "expert"), None),
        P(("dp", "expert"), None),
        P(("dp", "expert"), None),
        P(("dp", "expert"), None),
        P(None, "expert", None),
        P("expert", None),
    )
    out_specs = (
        P(("dp", "expert"), None),
        P(("dp", "expert"), None),
        P(None, ("expert", "dp"), None),
        P(("expert", "dp"), None),
    )
    return jax.shard_map(
        step, mesh=mesh, in_specs=in_specs, out_specs=out_specs, check_vma=False
    )
```
